128 devices in a mesh: ctx: 32 (over z_lo, x, y), tp: 4 (over z_hi, core).
Axes of the slice: x: 4, y: 4, z: 4 (z_hi: 2, z_lo: 2; z = z_hi * 2 + z_lo), core: 2. Of those that a mesh axis runs over, the one named last changes fastest.
Arguments:
- queries: bfloat16 [8192, 4096], P('ctx', 'tp'), may hold values from -6 to 6
- attn_keys: bfloat16 [8192, 4096], P('ctx', 'tp'), may hold values from -6 to 6
- attn_values: bfloat16 [8192, 4096], P('ctx', 'tp'), may hold values from -6 to 6
- out_proj: bfloat16 [4096, 8192], P('tp'), may hold values from -0.25 to 0.25
Outputs:
- mixed: bfloat16 [8192, 8192], P('ctx', 'tp')
The draws below stay inside these ranges and needn't reach their ends.
All inputs are finite; a program needn't handle non-finite values.
Results may differ from the reference program's by a relative error of at most 0.013.
Values may be sent and summed in bfloat16 or wider, within the bound.
A program may use at most 256 MiB of HBM per device.

```python
import jax
import jax.numpy as jnp
from jax import lax

D = 8192
HEADS = 32
HS = 128
HALF = 128
SEQ = 8192
INNER = 4096
N_CTX = 32
N_TP = 4


def draw_queries(key, part):
    base_key = jax.random.fold_in(key, 11)
    values = jnp.clip(1.6 * jax.random.normal(base_key, (SEQ, HEADS * HS), jnp.float32), -6.0, 6.0)
    return values.astype(jnp.bfloat16)


def draw_attn_keys(key, part):
    base_key = jax.random.fold_in(key, 13)
    values = jnp.clip(1.6 * jax.random.normal(base_key, (SEQ, HEADS * HS), jnp.float32), -6.0, 6.0)
    return values.astype(jnp.bfloat16)


def block_levels(stream_key, dims, cuts, smallest, high):
    factor_of, own = 1.0, jax.random.fold_in(stream_key, 6)
    for axis_at, blocks in cuts:
        draws = jnp.exp(jax.random.uniform(jax.random.fold_in(own, axis_at), (blocks,), jnp.float32, smallest / len(cuts), high / len(cuts)))
        factor_of = factor_of * jnp.repeat(draws, dims[axis_at] // blocks).reshape([-1 if axis == axis_at else 1 for axis in range(len(dims))])
    return factor_of


def scatter_about(own_key, dims, spread, most, split=(), kind=jnp.bfloat16):
    factor_of = block_levels(own_key, dims, split, -0.22, 0.18) if split else 1.0
    values = jax.random.normal(own_key, dims, jnp.float32) * spread * factor_of
    return jnp.minimum(jnp.maximum(values, -most), most).astype(kind)


def setup_inputs(seed: int = 0) -> dict:
    key_of = jax.random.split(jax.random.key(seed), 5)
    return {
        "queries": draw_queries(jax.random.fold_in(key_of[4], 71), 0),
        "attn_keys": draw_attn_keys(jax.random.fold_in(key_of[4], 71), 0),
        "attn_values": scatter_about(key_of[2], (SEQ, INNER), 1.0, 6.0, ((0, 32), (1, 4))),
        "out_proj": scatter_about(key_of[3], (INNER, D), (INNER // 9) ** -0.5, 0.25, ((0, 4),)),
    }


def block_order():
    blocks = jnp.arange(2 * N_CTX, dtype=jnp.int32)
    device = blocks // 2
    seq_block = jnp.where(blocks % 2 == 0, device, 2 * N_CTX - 1 - device).astype(jnp.int32)
    return seq_block


def reference(queries, attn_keys, attn_values, out_proj):
    seq_block = block_order()
    position = (seq_block[:, None] * HALF + jnp.arange(HALF, dtype=jnp.int32)[None, :]).reshape(-1).astype(jnp.int32)
    scale = 1.0 / (HS ** 0.5)
    visible = position[None, :] <= position[:, None]

    def one_head(operands):
        query_head, key_head, value_head = operands
        scores = jnp.dot(query_head.astype(jnp.float32), key_head.astype(jnp.float32).T,
                         precision=lax.Precision.HIGHEST) * scale
        top = jnp.max(jnp.where(visible, scores, -jnp.inf), axis=1, keepdims=True)
        weights = jnp.where(visible, jnp.exp(scores - top), 0.0)
        total = jnp.sum(weights, axis=1, keepdims=True)
        rounded = weights.astype(jnp.bfloat16).astype(jnp.float32)
        return jnp.dot(rounded, value_head.astype(jnp.float32), precision=lax.Precision.HIGHEST) / total

    def by_heads(array):
        return jnp.transpose(array.reshape(SEQ, HEADS, HS), (1, 0, 2))

    attended = lax.map(one_head, (by_heads(queries), by_heads(attn_keys), by_heads(attn_values)))
    attended = jnp.transpose(attended, (1, 0, 2)).reshape(SEQ, HEADS * HS).astype(jnp.bfloat16)
    group_cols = HEADS * HS // N_TP
    mixed = jnp.zeros((SEQ, out_proj.shape[1]), jnp.float32)
    for group in range(N_TP):
        part_cols = attended[:, group * group_cols:(group + 1) * group_cols]
        part_rows = out_proj[group * group_cols:(group + 1) * group_cols]
        partial_value = jnp.dot(part_cols, part_rows, preferred_element_type=jnp.float32).astype(jnp.bfloat16)
        mixed = mixed + partial_value.astype(jnp.float32)
    return mixed.astype(jnp.bfloat16)
```

```python
import functools

import jax
import jax.numpy as jnp
from jax import lax
from jax.experimental import pallas as pl
from jax.experimental.pallas import tpu as pltpu
from jax.sharding import PartitionSpec as P

MESH = pl.DeviceIdType.MESH
HS = 128
BLK = 128
GRP = 512
SCALE = 1.4426950408889634 / HS**0.5
LOW = -1e30


def attend_kernel(
    q_in, k_in, v_in, att_out,
    qbuf, kbuf, vbuf, m_ref, l_ref, acc_ref, obuf,
    xch_send, xch_recv, ring_send, ring_recv, ret_send, ret_recv,
):
    ctx = lax.axis_index("ctx")
    tp = lax.axis_index("tp")
    core = lax.rem(tp, 2)
    z, a, b = ctx // 16, lax.rem(ctx // 4, 4), lax.rem(ctx, 4)
    r = jnp.where(core == 0, a, b)
    w = jnp.where(core == 0, b, a)

    def device(z_at, r_at, w_at):
        at = z_at * 16 + jnp.where(core == 0, r_at * 4 + w_at, w_at * 4 + r_at)
        return (at, tp)

    left = device(z, lax.rem(r + 3, 4), w)
    right = device(z, lax.rem(r + 1, 4), w)
    spread = [(dz, dw) for dz in range(2) for dw in range(4)]

    def spread_at(dz, dw):
        return lax.rem(z + dz, 2), lax.rem(w + dw, 4)

    barrier = pltpu.get_barrier_semaphore()
    for dz, dw in spread[1:]:
        z_at, w_at = spread_at(dz, dw)
        pl.semaphore_signal(barrier, inc=1, device_id=device(z_at, r, w_at), device_id_type=MESH)
    for peer in (left, right):
        pl.semaphore_signal(barrier, inc=1, device_id=peer, device_id_type=MESH)
    pl.semaphore_wait(barrier, len(spread) + 1)

    ins = (q_in, k_in, v_in)

    def exchange(kind, half):
        group = z if half == 0 else 3 - z
        slot = w if half == 0 else 3 - w
        base = group * GRP + slot * BLK
        if kind > 0:
            base = base + r * (4 * GRP)
        dst = (qbuf, kbuf, vbuf)[kind].at[pl.ds(pl.multiple_of(base, BLK), BLK), :]
        for dz, dw in spread[1:] + spread[:1]:
            z_at, w_at = spread_at(dz, dw)
            column = pl.multiple_of((z_at * 4 + w_at) * HS, HS)
            src = ins[kind].at[pl.ds(half * BLK, BLK), pl.ds(column, HS)]
            if (dz, dw) == (0, 0):
                pltpu.make_async_copy(src, dst, xch_recv.at[kind, group]).start()
            else:
                pltpu.make_async_remote_copy(
                    src_ref=src, dst_ref=dst,
                    send_sem=xch_send.at[kind, half], recv_sem=xch_recv.at[kind, group],
                    device_id=device(z_at, r, w_at), device_id_type=MESH,
                ).start()

    def exchange_sent(kind, half):
        ref = ins[kind].at[pl.ds(half * BLK, BLK), pl.ds(0, 7 * HS)]
        pltpu.make_async_copy(ref, ref, xch_send.at[kind, half]).wait()

    def chunk(buf, r_at, group):
        return buf.at[pl.ds(pl.multiple_of(r_at * (4 * GRP) + group * GRP, GRP), GRP), :]

    def exchanged(kind, group):
        buf = (qbuf, kbuf, vbuf)[kind]
        ref = chunk(buf, r if kind > 0 else 0, group)
        pltpu.make_async_copy(ref, ref, xch_recv.at[kind, group]).wait()

    def ring_copy(kind, group, way, send_at, r_at, peer):
        ref = chunk((kbuf, vbuf)[kind], r_at, group)
        return pltpu.make_async_remote_copy(
            src_ref=ref, dst_ref=ref,
            send_sem=ring_send.at[group, kind, send_at], recv_sem=ring_recv.at[group, kind, way],
            device_id=peer, device_id_type=MESH,
        )

    def ring_start(group):
        for kind in range(2):
            ring_copy(kind, group, 0, 0, r, right).start()
            ring_copy(kind, group, 1, 1, r, left).start()

    r_left, r_right, r_far = lax.rem(r + 3, 4), lax.rem(r + 1, 4), lax.rem(r + 2, 4)

    def ring_wait(kind, group, way):
        r_at = (r_left, r_right, r_far)[way]
        ref = chunk((kbuf, vbuf)[kind], r_at, group)
        pltpu.make_async_copy(ref, ref, ring_recv.at[group, kind, way]).wait()

    def ring_near(group):
        ring_wait(0, group, 0)
        ring_copy(0, group, 2, 2, r_left, right).start()
        ring_wait(1, group, 1)
        ring_copy(1, group, 2, 2, r_right, left).start()
        ring_wait(1, group, 0)
        ring_wait(0, group, 1)

    def ring_far(group):
        ring_wait(0, group, 2)
        ring_wait(1, group, 2)

    def tile(q_group, r_at, k_group, size, mask=None):
        rows = pl.ds(pl.multiple_of(q_group * GRP, GRP), GRP)
        keys = pl.ds(pl.multiple_of(r_at * (4 * GRP) + k_group * GRP, GRP), size)
        scores = lax.dot_general(
            qbuf[rows, :], kbuf[keys, :], (((1,), (1,)), ((), ())), preferred_element_type=jnp.float32
        )
        if mask is not None:
            scores = jnp.where(mask, scores, LOW)
        old = m_ref[rows, :]
        new = jnp.maximum(old, jnp.max(scores, axis=1, keepdims=True))
        m_ref[rows, :] = new
        keep = jnp.exp2((old - new) * SCALE)
        shift = new * SCALE
        weights = jnp.exp2(scores * SCALE - jnp.concatenate([shift] * (size // HS), axis=1))
        total = weights[:, :HS]
        for at in range(1, size // HS):
            total = total + weights[:, at * HS:(at + 1) * HS]
        l_ref[rows, :] = l_ref[rows, :] * keep + total
        acc_ref[rows, :] = acc_ref[rows, :] * keep + jnp.dot(
            weights.astype(jnp.bfloat16), vbuf[keys, :], preferred_element_type=jnp.float32
        )

    def own_tile(group):
        row = lax.broadcasted_iota(jnp.int32, (GRP, GRP), 0)
        column = lax.broadcasted_iota(jnp.int32, (GRP, GRP), 1)
        tile(group, r, group, GRP, column <= row)

    def other_tile(group, r_at):
        before = jnp.where((r_at < r) == (group < 2), 1, 0)

        @pl.when((core == 1) | (before == 1))
        def _():
            row = lax.broadcasted_iota(jnp.int32, (GRP, GRP), 0) // BLK
            column = lax.broadcasted_iota(jnp.int32, (GRP, GRP), 1) // BLK
            count = row * jnp.where(core == 0, 0, 1) + jnp.where(core == 0, 4, 1) * before
            tile(group, r_at, group, GRP, column < count)

    def low_keys(r_at):
        @pl.loop(2, 4)
        def _(group):
            tile(group, r_at, 0, 2 * GRP)

    def finish(group):
        rows = pl.ds(group * GRP, GRP)
        total = jnp.sum(l_ref[rows, :], axis=1, keepdims=True)
        obuf[rows, :] = (acc_ref[rows, :] / total).astype(jnp.bfloat16)
        half = group // 2
        z_at = group if half == 0 else 3 - group
        column = pl.multiple_of((z * 4 + w) * HS, HS)
        dst = att_out.at[pl.ds(half * BLK, BLK), pl.ds(column, HS)]
        for dw in (1, 2, 3, 0):
            w_at = lax.rem(w + dw, 4)
            slot = w_at if half == 0 else 3 - w_at
            src = obuf.at[pl.ds(pl.multiple_of(group * GRP + slot * BLK, BLK), BLK), :]

            def remote(src=src, w_at=w_at, dw=dw):
                return pltpu.make_async_remote_copy(
                    src_ref=src, dst_ref=dst,
                    send_sem=ret_send.at[group, dw], recv_sem=ret_recv.at[half],
                    device_id=device(z_at, r, w_at), device_id_type=MESH,
                )

            if dw == 0:
                @pl.when(z == z_at)
                def _():
                    pltpu.make_async_copy(src, dst, ret_recv.at[half]).start()

                @pl.when(z != z_at)
                def _():
                    remote().start()
            else:
                remote().start()

    def returned_sent(group):
        half = group // 2
        z_at = group if half == 0 else 3 - group
        for dw in range(4):
            ref = obuf.at[pl.ds(0, BLK), :]
            if dw == 0:
                @pl.when(z != z_at)
                def _():
                    pltpu.make_async_copy(ref, ref, ret_send.at[group, dw]).wait()
            else:
                pltpu.make_async_copy(ref, ref, ret_send.at[group, dw]).wait()

    exchange(1, 0)
    exchange(2, 0)
    exchange(0, 0)
    exchange(0, 1)
    exchange(1, 1)
    exchange(2, 1)

    m_ref[...] = jnp.full_like(m_ref, LOW)
    l_ref[...] = jnp.zeros_like(l_ref)
    acc_ref[...] = jnp.zeros_like(acc_ref)

    for group in (0, 1):
        exchanged(1, group)
        exchanged(2, group)
        ring_start(group)
    exchanged(0, 0)
    exchanged(0, 1)
    own_tile(0)
    tile(1, r, 0, GRP)
    own_tile(1)
    exchanged(0, 2)
    exchanged(0, 3)
    for group in (2, 3):
        exchanged(1, group)
        exchanged(2, group)
        ring_start(group)
    low_keys(r)
    ring_near(0)
    ring_near(1)
    own_tile(2)
    tile(3, r, 2, GRP)
    own_tile(3)

    def low(r_at):
        other_tile(0, r_at)
        tile(1, r_at, 0, GRP)
        other_tile(1, r_at)
        low_keys(r_at)

    @pl.loop(0, 2)
    def _(at):
        low(lax.rem(r + 3 + 2 * at, 4))

    ring_near(2)
    ring_near(3)
    ring_far(0)
    ring_far(1)
    low(r_far)
    finish(0)
    finish(1)

    @pl.loop(0, 2)
    def _(at):
        r_at = lax.rem(r + 3 + 2 * at, 4)
        other_tile(2, r_at)
        tile(3, r_at, 2, GRP)

    ring_far(2)
    other_tile(2, r_far)
    finish(2)
    tile(3, r_far, 2, GRP)

    @pl.loop(0, 2)
    def _(at):
        other_tile(3, lax.rem(r + 3 + 2 * at, 4))

    ring_far(3)
    other_tile(3, r_far)
    finish(3)

    for half in range(2):
        ref = att_out.at[pl.ds(half * BLK, BLK), :]
        pltpu.make_async_copy(ref, ref, ret_recv.at[half]).wait()
    for kind in range(3):
        for half in range(2):
            exchange_sent(kind, half)
    for group in range(4):
        returned_sent(group)
        for kind in range(2):
            for at in range(3):
                ref = chunk(kbuf, 0, group)
                pltpu.make_async_copy(ref, ref, ring_send.at[group, kind, at]).wait()


def body(queries, attn_keys, attn_values, out_proj):
    tokens, inner = queries.shape
    any_spec = pl.BlockSpec(memory_space=pl.ANY)
    attended = pl.pallas_call(
        attend_kernel,
        out_shape=jax.ShapeDtypeStruct((tokens, inner), jnp.bfloat16),
        in_specs=[any_spec] * 3,
        out_specs=any_spec,
        scratch_shapes=[
            pltpu.VMEM((4 * GRP, HS), jnp.bfloat16),
            pltpu.VMEM((16 * GRP, HS), jnp.bfloat16),
            pltpu.VMEM((16 * GRP, HS), jnp.bfloat16),
            pltpu.VMEM((4 * GRP, HS), jnp.float32),
            pltpu.VMEM((4 * GRP, HS), jnp.float32),
            pltpu.VMEM((4 * GRP, HS), jnp.float32),
            pltpu.VMEM((4 * GRP, HS), jnp.bfloat16),
            pltpu.SemaphoreType.DMA((3, 2)),
            pltpu.SemaphoreType.DMA((3, 4)),
            pltpu.SemaphoreType.DMA((4, 2, 3)),
            pltpu.SemaphoreType.DMA((4, 2, 3)),
            pltpu.SemaphoreType.DMA((4, 4)),
            pltpu.SemaphoreType.DMA((2,)),
        ],
        compiler_params=pltpu.CompilerParams(
            collective_id=0, has_side_effects=True, vmem_limit_bytes=48 * 2**20
        ),
    )(queries, attn_keys, attn_values)
    partial_value = jnp.dot(attended, out_proj, preferred_element_type=jnp.float32).astype(jnp.bfloat16)
    return lax.psum_scatter(partial_value, "tp", scatter_dimension=1, tiled=True)


def solution(mesh):
    in_specs = (P("ctx", "tp"), P("ctx", "tp"), P("ctx", "tp"), P("tp", None))
    out_specs = P("ctx", "tp")
    return jax.shard_map(body, mesh=mesh, in_specs=in_specs, out_specs=out_specs, check_vma=False)
```

```python
import functools

import jax
import jax.numpy as jnp
from jax import lax
from jax.experimental import pallas as pl
from jax.experimental.pallas import tpu as pltpu
from jax.sharding import PartitionSpec as P

MESH = pl.DeviceIdType.MESH
HS = 128
BLK = 128
GRP = 512
SCALE = 1.4426950408889634 / HS**0.5
LOW = -1e30
OUT = 2048
PIECE = 1024
PIECES = OUT // PIECE


def block_kernel(
    q_in, k_in, v_in, w_in, out_ref,
    qbuf, kbuf, vbuf, m_ref, l_ref, acc_ref, obuf, att, wbuf, give, got, far_give, far_got, home,
    xch_send, xch_recv, ring_send, ring_recv, ret_send, ret_recv,
    give_send, give_recv, far_send, far_recv, w_sem,
):
    ctx = lax.axis_index("ctx")
    tp = lax.axis_index("tp")
    core = lax.rem(tp, 2)
    z, a, b = ctx // 16, lax.rem(ctx // 4, 4), lax.rem(ctx, 4)
    r = jnp.where(core == 0, a, b)
    w = jnp.where(core == 0, b, a)

    def device(z_at, r_at, w_at):
        at = z_at * 16 + jnp.where(core == 0, r_at * 4 + w_at, w_at * 4 + r_at)
        return (at, tp)

    left = device(z, lax.rem(r + 3, 4), w)
    right = device(z, lax.rem(r + 1, 4), w)
    spread = [(dz, dw) for dz in range(2) for dw in range(4)]

    def spread_at(dz, dw):
        return lax.rem(z + dz, 2), lax.rem(w + dw, 4)

    barrier = pltpu.get_barrier_semaphore()
    for dz, dw in spread[1:]:
        z_at, w_at = spread_at(dz, dw)
        pl.semaphore_signal(barrier, inc=1, device_id=device(z_at, r, w_at), device_id_type=MESH)
    for peer in (left, right):
        pl.semaphore_signal(barrier, inc=1, device_id=peer, device_id_type=MESH)
    twin = (ctx, tp + 1 - 2 * core)
    far = (ctx, lax.rem(tp + 2, 4))
    for peer in (twin, far):
        pl.semaphore_signal(barrier, inc=1, device_id=peer, device_id_type=MESH)
    pl.semaphore_wait(barrier, len(spread) + 3)

    ins = (q_in, k_in, v_in)

    def exchange(kind, half):
        group = z if half == 0 else 3 - z
        slot = w if half == 0 else 3 - w
        base = group * GRP + slot * BLK
        if kind > 0:
            base = base + r * (4 * GRP)
        dst = (qbuf, kbuf, vbuf)[kind].at[pl.ds(pl.multiple_of(base, BLK), BLK), :]
        for dz, dw in spread[1:] + spread[:1]:
            z_at, w_at = spread_at(dz, dw)
            column = pl.multiple_of((z_at * 4 + w_at) * HS, HS)
            src = ins[kind].at[pl.ds(half * BLK, BLK), pl.ds(column, HS)]
            if (dz, dw) == (0, 0):
                pltpu.make_async_copy(src, dst, xch_recv.at[kind, group]).start()
            else:
                pltpu.make_async_remote_copy(
                    src_ref=src, dst_ref=dst,
                    send_sem=xch_send.at[kind, half], recv_sem=xch_recv.at[kind, group],
                    device_id=device(z_at, r, w_at), device_id_type=MESH,
                ).start()

    def exchange_sent(kind, half):
        ref = ins[kind].at[pl.ds(half * BLK, BLK), pl.ds(0, 7 * HS)]
        pltpu.make_async_copy(ref, ref, xch_send.at[kind, half]).wait()

    def chunk(buf, r_at, group):
        return buf.at[pl.ds(pl.multiple_of(r_at * (4 * GRP) + group * GRP, GRP), GRP), :]

    def exchanged(kind, group):
        buf = (qbuf, kbuf, vbuf)[kind]
        ref = chunk(buf, r if kind > 0 else 0, group)
        pltpu.make_async_copy(ref, ref, xch_recv.at[kind, group]).wait()

    def ring_copy(kind, group, way, send_at, r_at, peer):
        ref = chunk((kbuf, vbuf)[kind], r_at, group)
        return pltpu.make_async_remote_copy(
            src_ref=ref, dst_ref=ref,
            send_sem=ring_send.at[group, kind, send_at], recv_sem=ring_recv.at[group, kind, way],
            device_id=peer, device_id_type=MESH,
        )

    def ring_start(group):
        for kind in range(2):
            ring_copy(kind, group, 0, 0, r, right).start()
            ring_copy(kind, group, 1, 1, r, left).start()

    r_left, r_right, r_far = lax.rem(r + 3, 4), lax.rem(r + 1, 4), lax.rem(r + 2, 4)

    def ring_wait(kind, group, way):
        r_at = (r_left, r_right, r_far)[way]
        ref = chunk((kbuf, vbuf)[kind], r_at, group)
        pltpu.make_async_copy(ref, ref, ring_recv.at[group, kind, way]).wait()

    def ring_near(group):
        ring_wait(0, group, 0)
        ring_copy(0, group, 2, 2, r_left, right).start()
        ring_wait(1, group, 1)
        ring_copy(1, group, 2, 2, r_right, left).start()
        ring_wait(1, group, 0)
        ring_wait(0, group, 1)

    def ring_far(group):
        ring_wait(0, group, 2)
        ring_wait(1, group, 2)

    def tile(q_group, r_at, k_group, size, mask=None):
        rows = pl.ds(pl.multiple_of(q_group * GRP, GRP), GRP)
        keys = pl.ds(pl.multiple_of(r_at * (4 * GRP) + k_group * GRP, GRP), size)
        scores = lax.dot_general(
            qbuf[rows, :], kbuf[keys, :], (((1,), (1,)), ((), ())), preferred_element_type=jnp.float32
        )
        if mask is not None:
            scores = jnp.where(mask, scores, LOW)
        old = m_ref[rows, :]
        new = jnp.maximum(old, jnp.max(scores, axis=1, keepdims=True))
        m_ref[rows, :] = new
        keep = jnp.exp2((old - new) * SCALE)
        shift = new * SCALE
        weights = jnp.exp2(scores * SCALE - jnp.concatenate([shift] * (size // HS), axis=1))
        total = weights[:, :HS]
        for at in range(1, size // HS):
            total = total + weights[:, at * HS:(at + 1) * HS]
        l_ref[rows, :] = l_ref[rows, :] * keep + total
        acc_ref[rows, :] = acc_ref[rows, :] * keep + jnp.dot(
            weights.astype(jnp.bfloat16), vbuf[keys, :], preferred_element_type=jnp.float32
        )

    def own_tile(group):
        row = lax.broadcasted_iota(jnp.int32, (GRP, GRP), 0)
        column = lax.broadcasted_iota(jnp.int32, (GRP, GRP), 1)
        tile(group, r, group, GRP, column <= row)

    def other_tile(group, r_at):
        before = jnp.where((r_at < r) == (group < 2), 1, 0)

        @pl.when((core == 1) | (before == 1))
        def _():
            row = lax.broadcasted_iota(jnp.int32, (GRP, GRP), 0) // BLK
            column = lax.broadcasted_iota(jnp.int32, (GRP, GRP), 1) // BLK
            count = row * jnp.where(core == 0, 0, 1) + jnp.where(core == 0, 4, 1) * before
            tile(group, r_at, group, GRP, column < count)

    def low_keys(r_at):
        @pl.loop(2, 4)
        def _(group):
            tile(group, r_at, 0, 2 * GRP)

    def finish(group):
        rows = pl.ds(group * GRP, GRP)
        total = jnp.sum(l_ref[rows, :], axis=1, keepdims=True)
        obuf[rows, :] = (acc_ref[rows, :] / total).astype(jnp.bfloat16)
        half = group // 2
        z_at = group if half == 0 else 3 - group
        column = pl.multiple_of((z * 4 + w) * HS, HS)
        dst = att.at[pl.ds(half * BLK, BLK), pl.ds(column, HS)]
        for dw in (1, 2, 3, 0):
            w_at = lax.rem(w + dw, 4)
            slot = w_at if half == 0 else 3 - w_at
            src = obuf.at[pl.ds(pl.multiple_of(group * GRP + slot * BLK, BLK), BLK), :]

            def remote(src=src, w_at=w_at, dw=dw):
                return pltpu.make_async_remote_copy(
                    src_ref=src, dst_ref=dst,
                    send_sem=ret_send.at[group, dw], recv_sem=ret_recv.at[half],
                    device_id=device(z_at, r, w_at), device_id_type=MESH,
                )

            if dw == 0:
                @pl.when(z == z_at)
                def _():
                    pltpu.make_async_copy(src, dst, ret_recv.at[half]).start()

                @pl.when(z != z_at)
                def _():
                    remote().start()
            else:
                remote().start()

    def returned_sent(group):
        half = group // 2
        z_at = group if half == 0 else 3 - group
        for dw in range(4):
            ref = obuf.at[pl.ds(0, BLK), :]
            if dw == 0:
                @pl.when(z != z_at)
                def _():
                    pltpu.make_async_copy(ref, ref, ret_send.at[group, dw]).wait()
            else:
                pltpu.make_async_copy(ref, ref, ret_send.at[group, dw]).wait()

    def project(half, tp_at, at):
        column = pl.multiple_of(tp_at * OUT + at * PIECE, PIECE)
        return jnp.dot(
            att[pl.ds(half * BLK, BLK), :], wbuf[:, pl.ds(column, PIECE)], preferred_element_type=jnp.float32
        )

    def piece(buf, *lead):
        *lead, at = lead
        return buf.at[(*lead, slice(None), pl.ds(pl.multiple_of(at * PIECE, PIECE), PIECE))]

    def give_copy(half, which, at):
        return pltpu.make_async_remote_copy(
            src_ref=piece(give, half, which, at), dst_ref=piece(got, half, which, at),
            send_sem=give_send.at[half, which, at], recv_sem=give_recv.at[half, which, at],
            device_id=twin, device_id_type=MESH,
        )

    def far_copy(half, at):
        return pltpu.make_async_remote_copy(
            src_ref=piece(far_give, half, at), dst_ref=piece(far_got, half, at),
            send_sem=far_send.at[half, at], recv_sem=far_recv.at[half, at],
            device_id=far, device_id_type=MESH,
        )

    def project_give(half, which):
        tp_at = lax.rem(twin[1] + (2 if which == 0 else 0), 4)

        @pl.loop(0, PIECES)
        def _(at):
            piece(give, half, which, at)[...] = project(half, tp_at, at).astype(jnp.bfloat16)
            give_copy(half, which, at).start()

    def project_far(half):
        @pl.loop(0, PIECES)
        def _(at):
            own = project(half, far[1], at)
            give_copy(half, 0, at).wait_recv()
            piece(far_give, half, at)[...] = (own + piece(got, half, 0, at)[...].astype(jnp.float32)).astype(jnp.bfloat16)
            far_copy(half, at).start()

    def project_home(half):
        @pl.loop(0, PIECES)
        def _(at):
            own = project(half, tp, at)
            give_copy(half, 1, at).wait_recv()
            piece(home, half, at)[...] = own + piece(got, half, 1, at)[...].astype(jnp.float32)

    def project_end(half):
        @pl.loop(0, PIECES)
        def _(at):
            far_copy(half, at).wait_recv()
            both = piece(home, half, at)[...] + piece(far_got, half, at)[...].astype(jnp.float32)
            columns = pl.ds(pl.multiple_of(at * PIECE, PIECE), PIECE)
            out_ref[pl.ds(half * BLK, BLK), columns] = both.astype(jnp.bfloat16)

    def returned(half):
        ref = att.at[pl.ds(half * BLK, BLK), :]
        pltpu.make_async_copy(ref, ref, ret_recv.at[half]).wait()

    exchange(1, 0)
    exchange(2, 0)
    exchange(0, 0)
    exchange(0, 1)
    exchange(1, 1)
    exchange(2, 1)
    load_w = pltpu.make_async_copy(w_in, wbuf, w_sem)
    load_w.start()

    m_ref[...] = jnp.full_like(m_ref, LOW)
    l_ref[...] = jnp.zeros_like(l_ref)
    acc_ref[...] = jnp.zeros_like(acc_ref)

    def low(r_at):
        other_tile(0, r_at)
        tile(1, r_at, 0, GRP)
        other_tile(1, r_at)

    for group in (0, 1):
        exchanged(1, group)
        exchanged(2, group)
        ring_start(group)
    exchanged(0, 0)
    exchanged(0, 1)
    own_tile(0)
    tile(1, r, 0, GRP)
    own_tile(1)
    exchanged(0, 2)
    exchanged(0, 3)
    ring_near(0)
    low_keys(r)
    ring_near(1)
    for group in (2, 3):
        exchanged(1, group)
        exchanged(2, group)
        ring_start(group)

    @pl.loop(0, 2)
    def _(at):
        low(lax.rem(r + 3 + 2 * at, 4))

    low_keys(r_left)
    ring_far(0)
    ring_far(1)
    low(r_far)
    finish(0)
    finish(1)
    low_keys(r_right)
    ring_near(2)
    ring_near(3)
    low_keys(r_far)
    load_w.wait()
    returned(0)
    project_give(0, 0)
    project_far(0)
    project_give(0, 1)
    project_home(0)
    own_tile(2)
    tile(3, r, 2, GRP)
    own_tile(3)

    @pl.loop(0, 2)
    def _(at):
        r_at = lax.rem(r + 3 + 2 * at, 4)
        other_tile(2, r_at)
        tile(3, r_at, 2, GRP)

    ring_far(2)
    other_tile(2, r_far)
    finish(2)
    tile(3, r_far, 2, GRP)

    @pl.loop(0, 2)
    def _(at):
        other_tile(3, lax.rem(r + 3 + 2 * at, 4))

    ring_far(3)
    other_tile(3, r_far)
    finish(3)
    project_end(0)
    returned(1)
    project_give(1, 0)
    project_far(1)
    project_give(1, 1)
    project_home(1)
    project_end(1)

    for kind in range(3):
        for half in range(2):
            exchange_sent(kind, half)
    for group in range(4):
        returned_sent(group)
        for kind in range(2):
            for at in range(3):
                ref = chunk(kbuf, 0, group)
                pltpu.make_async_copy(ref, ref, ring_send.at[group, kind, at]).wait()
    for half in range(2):
        for at in range(PIECES):
            give_copy(half, 0, at).wait_send()
            give_copy(half, 1, at).wait_send()
            far_copy(half, at).wait_send()


def body(queries, attn_keys, attn_values, out_proj):
    tokens, inner = queries.shape
    any_spec = pl.BlockSpec(memory_space=pl.ANY)
    return pl.pallas_call(
        block_kernel,
        out_shape=jax.ShapeDtypeStruct((tokens, OUT), jnp.bfloat16),
        in_specs=[any_spec] * 4,
        out_specs=pl.BlockSpec(memory_space=pltpu.VMEM),
        scratch_shapes=[
            pltpu.VMEM((4 * GRP, HS), jnp.bfloat16),
            pltpu.VMEM((16 * GRP, HS), jnp.bfloat16),
            pltpu.VMEM((16 * GRP, HS), jnp.bfloat16),
            pltpu.VMEM((4 * GRP, HS), jnp.float32),
            pltpu.VMEM((4 * GRP, HS), jnp.float32),
            pltpu.VMEM((4 * GRP, HS), jnp.float32),
            pltpu.VMEM((4 * GRP, HS), jnp.bfloat16),
            pltpu.VMEM((tokens, inner), jnp.bfloat16),
            pltpu.VMEM((inner, 4 * OUT), jnp.bfloat16),
            pltpu.VMEM((2, 2, BLK, OUT), jnp.bfloat16),
            pltpu.VMEM((2, 2, BLK, OUT), jnp.bfloat16),
            pltpu.VMEM((2, BLK, OUT), jnp.bfloat16),
            pltpu.VMEM((2, BLK, OUT), jnp.bfloat16),
            pltpu.VMEM((2, BLK, OUT), jnp.float32),
            pltpu.SemaphoreType.DMA((3, 2)),
            pltpu.SemaphoreType.DMA((3, 4)),
            pltpu.SemaphoreType.DMA((4, 2, 3)),
            pltpu.SemaphoreType.DMA((4, 2, 3)),
            pltpu.SemaphoreType.DMA((4, 4)),
            pltpu.SemaphoreType.DMA((2,)),
            pltpu.SemaphoreType.DMA((2, 2, PIECES)),
            pltpu.SemaphoreType.DMA((2, 2, PIECES)),
            pltpu.SemaphoreType.DMA((2, PIECES)),
            pltpu.SemaphoreType.DMA((2, PIECES)),
            pltpu.SemaphoreType.DMA,
        ],
        compiler_params=pltpu.CompilerParams(
            collective_id=0, has_side_effects=True, vmem_limit_bytes=60 * 2**20
        ),
    )(queries, attn_keys, attn_values, out_proj)


def solution(mesh):
    in_specs = (P("ctx", "tp"), P("ctx", "tp"), P("ctx", "tp"), P("tp", None))
    out_specs = P("ctx", "tp")
    return jax.shard_map(body, mesh=mesh, in_specs=in_specs, out_specs=out_specs, check_vma=False)
```

```python
import functools

import jax
import jax.numpy as jnp
from jax import lax
from jax.experimental import pallas as pl
from jax.experimental.pallas import tpu as pltpu
from jax.sharding import PartitionSpec as P

MESH = pl.DeviceIdType.MESH
HS = 128
BLK = 128
GRP = 512
SCALE = 1.4426950408889634 / HS**0.5
LOW = -1e30
OUT = 2048
PIECE = 1024
PIECES = OUT // PIECE


def block_kernel(
    q_in, k_in, v_in, w_in, out_ref,
    qbuf, kbuf, vbuf, m_ref, l_ref, acc_ref, obuf, att, wbuf, give, got, far_give, far_got, home,
    xch_send, xch_recv, ring_send, ring_recv, ret_send, ret_recv,
    give_send, give_recv, far_send, far_recv, w_sem,
):
    ctx = lax.axis_index("ctx")
    tp = lax.axis_index("tp")
    core = lax.rem(tp, 2)
    z, a, b = ctx // 16, lax.rem(ctx // 4, 4), lax.rem(ctx, 4)
    r = jnp.where(core == 0, a, b)
    w = jnp.where(core == 0, b, a)

    def device(z_at, r_at, w_at):
        at = z_at * 16 + jnp.where(core == 0, r_at * 4 + w_at, w_at * 4 + r_at)
        return (at, tp)

    left = device(z, lax.rem(r + 3, 4), w)
    right = device(z, lax.rem(r + 1, 4), w)
    spread = [(dz, dw) for dz in range(2) for dw in range(4)]

    def spread_at(dz, dw):
        return lax.rem(z + dz, 2), lax.rem(w + dw, 4)

    barrier = pltpu.get_barrier_semaphore()
    for dz, dw in spread[1:]:
        z_at, w_at = spread_at(dz, dw)
        pl.semaphore_signal(barrier, inc=1, device_id=device(z_at, r, w_at), device_id_type=MESH)
    for peer in (left, right):
        pl.semaphore_signal(barrier, inc=1, device_id=peer, device_id_type=MESH)
    twin = (ctx, tp + 1 - 2 * core)
    far = (ctx, lax.rem(tp + 2, 4))
    for peer in (twin, far):
        pl.semaphore_signal(barrier, inc=1, device_id=peer, device_id_type=MESH)
    pl.semaphore_wait(barrier, len(spread) + 3)

    ins = (q_in, k_in, v_in)

    def exchange(kind, half):
        group = z if half == 0 else 3 - z
        slot = w if half == 0 else 3 - w
        base = group * GRP + slot * BLK
        if kind > 0:
            base = base + r * (4 * GRP)
        dst = (qbuf, kbuf, vbuf)[kind].at[pl.ds(pl.multiple_of(base, BLK), BLK), :]
        for dz, dw in spread[4:] + spread[1:4] + spread[:1]:
            z_at, w_at = spread_at(dz, dw)
            column = pl.multiple_of((z_at * 4 + w_at) * HS, HS)
            src = ins[kind].at[pl.ds(half * BLK, BLK), pl.ds(column, HS)]
            if (dz, dw) == (0, 0):
                pltpu.make_async_copy(src, dst, xch_recv.at[kind, group]).start()
            else:
                pltpu.make_async_remote_copy(
                    src_ref=src, dst_ref=dst,
                    send_sem=xch_send.at[kind, half], recv_sem=xch_recv.at[kind, group],
                    device_id=device(z_at, r, w_at), device_id_type=MESH,
                ).start()

    def exchange_sent(kind, half):
        ref = ins[kind].at[pl.ds(half * BLK, BLK), pl.ds(0, 7 * HS)]
        pltpu.make_async_copy(ref, ref, xch_send.at[kind, half]).wait()

    def chunk(buf, r_at, group):
        return buf.at[pl.ds(pl.multiple_of(r_at * (4 * GRP) + group * GRP, GRP), GRP), :]

    def exchanged(kind, group):
        buf = (qbuf, kbuf, vbuf)[kind]
        ref = chunk(buf, r if kind > 0 else 0, group)
        pltpu.make_async_copy(ref, ref, xch_recv.at[kind, group]).wait()

    def ring_copy(kind, group, way, send_at, r_at, peer):
        ref = chunk((kbuf, vbuf)[kind], r_at, group)
        return pltpu.make_async_remote_copy(
            src_ref=ref, dst_ref=ref,
            send_sem=ring_send.at[group, kind, send_at], recv_sem=ring_recv.at[group, kind, way],
            device_id=peer, device_id_type=MESH,
        )

    def ring_start(group):
        for kind in range(2):
            ring_copy(kind, group, 0, 0, r, right).start()
            ring_copy(kind, group, 1, 1, r, left).start()

    r_left, r_right, r_far = lax.rem(r + 3, 4), lax.rem(r + 1, 4), lax.rem(r + 2, 4)

    def ring_wait(kind, group, way):
        r_at = (r_left, r_right, r_far)[way]
        ref = chunk((kbuf, vbuf)[kind], r_at, group)
        pltpu.make_async_copy(ref, ref, ring_recv.at[group, kind, way]).wait()

    def ring_near(group):
        ring_wait(0, group, 0)
        ring_copy(0, group, 2, 2, r_left, right).start()
        ring_wait(1, group, 1)
        ring_copy(1, group, 2, 2, r_right, left).start()
        ring_wait(1, group, 0)
        ring_wait(0, group, 1)

    def ring_far(group):
        ring_wait(0, group, 2)
        ring_wait(1, group, 2)

    def tile(q_group, r_at, k_group, size, mask=None, tall=1):
        rows = pl.ds(pl.multiple_of(q_group * GRP, GRP), tall * GRP)
        keys = pl.ds(pl.multiple_of(r_at * (4 * GRP) + k_group * GRP, GRP), size)
        scores = lax.dot_general(
            qbuf[rows, :], kbuf[keys, :], (((1,), (1,)), ((), ())), preferred_element_type=jnp.float32
        )
        if mask is not None:
            scores = jnp.where(mask, scores, LOW)
        old = m_ref[rows, :]
        new = jnp.maximum(old, jnp.max(scores, axis=1, keepdims=True))
        m_ref[rows, :] = new
        keep = jnp.exp2((old - new) * SCALE)
        shift = new * SCALE
        weights = jnp.exp2(scores * SCALE - jnp.concatenate([shift] * (size // HS), axis=1))
        total = weights[:, :HS]
        for at in range(1, size // HS):
            total = total + weights[:, at * HS:(at + 1) * HS]
        l_ref[rows, :] = l_ref[rows, :] * keep + total
        acc_ref[rows, :] = acc_ref[rows, :] * keep + jnp.dot(
            weights.astype(jnp.bfloat16), vbuf[keys, :], preferred_element_type=jnp.float32
        )

    def own_tile(group):
        row = lax.broadcasted_iota(jnp.int32, (GRP, GRP), 0)
        column = lax.broadcasted_iota(jnp.int32, (GRP, GRP), 1)
        tile(group, r, group, GRP, column <= row)

    def other_tile(group, r_at):
        before = jnp.where((r_at < r) == (group < 2), 1, 0)

        @pl.when((core == 1) | (before == 1))
        def _():
            row = lax.broadcasted_iota(jnp.int32, (GRP, GRP), 0) // BLK
            column = lax.broadcasted_iota(jnp.int32, (GRP, GRP), 1) // BLK
            count = row * jnp.where(core == 0, 0, 1) + jnp.where(core == 0, 4, 1) * before
            tile(group, r_at, group, GRP, column < count)

    def low_keys(r_at):
        tile(2, r_at, 0, 2 * GRP, tall=2)

    def finish(group):
        rows = pl.ds(group * GRP, GRP)
        total = jnp.sum(l_ref[rows, :], axis=1, keepdims=True)
        obuf[rows, :] = (acc_ref[rows, :] / total).astype(jnp.bfloat16)
        half = group // 2
        z_at = group if half == 0 else 3 - group
        column = pl.multiple_of((z * 4 + w) * HS, HS)
        dst = att.at[pl.ds(half * BLK, BLK), pl.ds(column, HS)]
        for dw in (1, 2, 3, 0):
            w_at = lax.rem(w + dw, 4)
            slot = w_at if half == 0 else 3 - w_at
            src = obuf.at[pl.ds(pl.multiple_of(group * GRP + slot * BLK, BLK), BLK), :]

            def remote(src=src, w_at=w_at, dw=dw):
                return pltpu.make_async_remote_copy(
                    src_ref=src, dst_ref=dst,
                    send_sem=ret_send.at[group, dw], recv_sem=ret_recv.at[half],
                    device_id=device(z_at, r, w_at), device_id_type=MESH,
                )

            if dw == 0:
                @pl.when(z == z_at)
                def _():
                    pltpu.make_async_copy(src, dst, ret_recv.at[half]).start()

                @pl.when(z != z_at)
                def _():
                    remote().start()
            else:
                remote().start()

    def returned_sent(group):
        half = group // 2
        z_at = group if half == 0 else 3 - group
        for dw in range(4):
            ref = obuf.at[pl.ds(0, BLK), :]
            if dw == 0:
                @pl.when(z != z_at)
                def _():
                    pltpu.make_async_copy(ref, ref, ret_send.at[group, dw]).wait()
            else:
                pltpu.make_async_copy(ref, ref, ret_send.at[group, dw]).wait()

    def project(half, tp_at, at):
        column = pl.multiple_of(tp_at * OUT + at * PIECE, PIECE)
        return jnp.dot(
            att[pl.ds(half * BLK, BLK), :], wbuf[:, pl.ds(column, PIECE)], preferred_element_type=jnp.float32
        )

    def piece(buf, *lead):
        *lead, at = lead
        return buf.at[(*lead, slice(None), pl.ds(pl.multiple_of(at * PIECE, PIECE), PIECE))]

    def give_copy(half, which, at):
        return pltpu.make_async_remote_copy(
            src_ref=piece(give, half, which, at), dst_ref=piece(got, half, which, at),
            send_sem=give_send.at[half, which, at], recv_sem=give_recv.at[half, which, at],
            device_id=twin, device_id_type=MESH,
        )

    def far_copy(half, at):
        return pltpu.make_async_remote_copy(
            src_ref=piece(far_give, half, at), dst_ref=piece(far_got, half, at),
            send_sem=far_send.at[half, at], recv_sem=far_recv.at[half, at],
            device_id=far, device_id_type=MESH,
        )

    def project_give(half, which):
        tp_at = lax.rem(twin[1] + (2 if which == 0 else 0), 4)

        @pl.loop(0, PIECES)
        def _(at):
            piece(give, half, which, at)[...] = project(half, tp_at, at).astype(jnp.bfloat16)
            give_copy(half, which, at).start()

    def project_far(half):
        @pl.loop(0, PIECES)
        def _(at):
            own = project(half, far[1], at)
            give_copy(half, 0, at).wait_recv()
            piece(far_give, half, at)[...] = (own + piece(got, half, 0, at)[...].astype(jnp.float32)).astype(jnp.bfloat16)
            far_copy(half, at).start()

    def project_home(half):
        @pl.loop(0, PIECES)
        def _(at):
            own = project(half, tp, at)
            give_copy(half, 1, at).wait_recv()
            piece(home, half, at)[...] = own + piece(got, half, 1, at)[...].astype(jnp.float32)

    def project_end(half):
        @pl.loop(0, PIECES)
        def _(at):
            far_copy(half, at).wait_recv()
            both = piece(home, half, at)[...] + piece(far_got, half, at)[...].astype(jnp.float32)
            columns = pl.ds(pl.multiple_of(at * PIECE, PIECE), PIECE)
            out_ref[pl.ds(half * BLK, BLK), columns] = both.astype(jnp.bfloat16)

    def returned(half):
        ref = att.at[pl.ds(half * BLK, BLK), :]
        pltpu.make_async_copy(ref, ref, ret_recv.at[half]).wait()

    exchange(1, 0)
    exchange(2, 0)
    load_w = pltpu.make_async_copy(w_in, wbuf, w_sem)
    load_w.start()

    m_ref[...] = jnp.full_like(m_ref, LOW)
    l_ref[...] = jnp.zeros_like(l_ref)
    acc_ref[...] = jnp.zeros_like(acc_ref)

    def exchanged_start(group):
        exchanged(1, group)
        exchanged(2, group)
        ring_start(group)

    def low(r_at):
        other_tile(0, r_at)
        tile(1, r_at, 0, GRP)
        other_tile(1, r_at)

    def high(r_at):
        other_tile(2, r_at)
        tile(3, r_at, 2, GRP)
        other_tile(3, r_at)

    first, second, third, fourth = z, 1 - z, 3 - z, 2 + z

    exchanged_start(first)
    exchange(0, 0)
    exchanged_start(second)
    exchange(1, 1)
    exchange(2, 1)
    exchanged(0, 0)
    exchanged(0, 1)
    exchange(0, 1)
    own_tile(0)
    tile(1, r, 0, GRP)
    own_tile(1)
    ring_near(first)
    ring_near(second)
    exchanged_start(third)

    @pl.loop(0, 2)
    def _(at):
        low(lax.rem(r + 3 + 2 * at, 4))

    exchanged_start(fourth)
    ring_far(first)
    ring_far(second)
    low(r_far)
    finish(0)
    finish(1)
    exchanged(0, 2)
    exchanged(0, 3)

    @pl.loop(0, 2)
    def _(at):
        low_keys(lax.rem(r + 3 * at, 4))

    ring_near(third)

    @pl.loop(0, 2)
    def _(at):
        low_keys(lax.rem(r + 1 + at, 4))

    ring_near(fourth)
    load_w.wait()
    returned(0)
    project_give(0, 0)
    project_far(0)
    own_tile(2)
    tile(3, r, 2, GRP)
    own_tile(3)

    @pl.loop(0, 2)
    def _(at):
        high(lax.rem(r + 3 + 2 * at, 4))

    project_give(0, 1)
    project_home(0)
    ring_far(third)
    ring_far(fourth)
    high(r_far)
    finish(2)
    finish(3)
    project_end(0)
    returned(1)
    project_give(1, 0)
    project_far(1)
    project_give(1, 1)
    project_home(1)
    project_end(1)

    for kind in range(3):
        for half in range(2):
            exchange_sent(kind, half)
    for group in range(4):
        returned_sent(group)
        for kind in range(2):
            for at in range(3):
                ref = chunk(kbuf, 0, group)
                pltpu.make_async_copy(ref, ref, ring_send.at[group, kind, at]).wait()
    for half in range(2):
        for at in range(PIECES):
            give_copy(half, 0, at).wait_send()
            give_copy(half, 1, at).wait_send()
            far_copy(half, at).wait_send()


def body(queries, attn_keys, attn_values, out_proj):
    tokens, inner = queries.shape
    any_spec = pl.BlockSpec(memory_space=pl.ANY)
    return pl.pallas_call(
        block_kernel,
        out_shape=jax.ShapeDtypeStruct((tokens, OUT), jnp.bfloat16),
        in_specs=[any_spec] * 4,
        out_specs=pl.BlockSpec(memory_space=pltpu.VMEM),
        scratch_shapes=[
            pltpu.VMEM((4 * GRP, HS), jnp.bfloat16),
            pltpu.VMEM((16 * GRP, HS), jnp.bfloat16),
            pltpu.VMEM((16 * GRP, HS), jnp.bfloat16),
            pltpu.VMEM((4 * GRP, HS), jnp.float32),
            pltpu.VMEM((4 * GRP, HS), jnp.float32),
            pltpu.VMEM((4 * GRP, HS), jnp.float32),
            pltpu.VMEM((4 * GRP, HS), jnp.bfloat16),
            pltpu.VMEM((tokens, inner), jnp.bfloat16),
            pltpu.VMEM((inner, 4 * OUT), jnp.bfloat16),
            pltpu.VMEM((2, 2, BLK, OUT), jnp.bfloat16),
            pltpu.VMEM((2, 2, BLK, OUT), jnp.bfloat16),
            pltpu.VMEM((2, BLK, OUT), jnp.bfloat16),
            pltpu.VMEM((2, BLK, OUT), jnp.bfloat16),
            pltpu.VMEM((2, BLK, OUT), jnp.float32),
            pltpu.SemaphoreType.DMA((3, 2)),
            pltpu.SemaphoreType.DMA((3, 4)),
            pltpu.SemaphoreType.DMA((4, 2, 3)),
            pltpu.SemaphoreType.DMA((4, 2, 3)),
            pltpu.SemaphoreType.DMA((4, 4)),
            pltpu.SemaphoreType.DMA((2,)),
            pltpu.SemaphoreType.DMA((2, 2, PIECES)),
            pltpu.SemaphoreType.DMA((2, 2, PIECES)),
            pltpu.SemaphoreType.DMA((2, PIECES)),
            pltpu.SemaphoreType.DMA((2, PIECES)),
            pltpu.SemaphoreType.DMA,
        ],
        compiler_params=pltpu.CompilerParams(
            collective_id=0, has_side_effects=True, vmem_limit_bytes=60 * 2**20
        ),
    )(queries, attn_keys, attn_values, out_proj)


def solution(mesh):
    in_specs = (P("ctx", "tp"), P("ctx", "tp"), P("ctx", "tp"), P("tp", None))
    out_specs = P("ctx", "tp")
    return jax.shard_map(body, mesh=mesh, in_specs=in_specs, out_specs=out_specs, check_vma=False)
```

```python
import functools

import jax
import jax.numpy as jnp
from jax import lax
from jax.experimental import pallas as pl
from jax.experimental.pallas import tpu as pltpu
from jax.sharding import PartitionSpec as P

MESH = pl.DeviceIdType.MESH
HS = 128
BLK = 128
GRP = 512
SCALE = 1.4426950408889634 / HS**0.5
LOW = -1e30
OUT = 2048
PIECE = 1024
PIECES = OUT // PIECE


def block_kernel(
    q_in, k_in, v_in, w_in, out_ref,
    qbuf, kbuf, vbuf, m_ref, l_ref, acc_ref, obuf, att, wbuf, give, got, far_give, far_got, home,
    xch_send, xch_recv, ring_send, ring_recv, ret_send, ret_recv,
    give_send, give_recv, far_send, far_recv, w_sem,
):
    ctx = lax.axis_index("ctx")
    tp = lax.axis_index("tp")
    core = lax.rem(tp, 2)
    z, a, b = ctx // 16, lax.rem(ctx // 4, 4), lax.rem(ctx, 4)
    r = jnp.where(core == 0, a, b)
    w = jnp.where(core == 0, b, a)

    def device(z_at, r_at, w_at):
        at = z_at * 16 + jnp.where(core == 0, r_at * 4 + w_at, w_at * 4 + r_at)
        return (at, tp)

    left = device(z, lax.rem(r + 3, 4), w)
    right = device(z, lax.rem(r + 1, 4), w)
    spread = [(dz, dw) for dz in range(2) for dw in range(4)]

    def spread_at(dz, dw):
        return lax.rem(z + dz, 2), lax.rem(w + dw, 4)

    barrier = pltpu.get_barrier_semaphore()
    for dz, dw in spread[1:]:
        z_at, w_at = spread_at(dz, dw)
        pl.semaphore_signal(barrier, inc=1, device_id=device(z_at, r, w_at), device_id_type=MESH)
    for peer in (left, right):
        pl.semaphore_signal(barrier, inc=1, device_id=peer, device_id_type=MESH)
    twin = (ctx, tp + 1 - 2 * core)
    far = (ctx, lax.rem(tp + 2, 4))
    for peer in (twin, far):
        pl.semaphore_signal(barrier, inc=1, device_id=peer, device_id_type=MESH)
    pl.semaphore_wait(barrier, len(spread) + 3)

    ins = (q_in, k_in, v_in)

    def exchange(kind, half):
        group = z if half == 0 else 3 - z
        slot = w if half == 0 else 3 - w
        base = group * GRP + slot * BLK
        if kind > 0:
            base = base + r * (4 * GRP)
        dst = (qbuf, kbuf, vbuf)[kind].at[pl.ds(pl.multiple_of(base, BLK), BLK), :]
        for dz, dw in spread[4:] + spread[1:4] + spread[:1]:
            z_at, w_at = spread_at(dz, dw)
            column = pl.multiple_of((z_at * 4 + w_at) * HS, HS)
            src = ins[kind].at[pl.ds(half * BLK, BLK), pl.ds(column, HS)]
            if (dz, dw) == (0, 0):
                pltpu.make_async_copy(src, dst, xch_recv.at[kind, group]).start()
            else:
                pltpu.make_async_remote_copy(
                    src_ref=src, dst_ref=dst,
                    send_sem=xch_send.at[kind, half], recv_sem=xch_recv.at[kind, group],
                    device_id=device(z_at, r, w_at), device_id_type=MESH,
                ).start()

    def exchange_sent(kind, half):
        ref = ins[kind].at[pl.ds(half * BLK, BLK), pl.ds(0, 7 * HS)]
        pltpu.make_async_copy(ref, ref, xch_send.at[kind, half]).wait()

    def chunk(buf, r_at, group):
        return buf.at[pl.ds(pl.multiple_of(r_at * (4 * GRP) + group * GRP, GRP), GRP), :]

    def exchanged(kind, group):
        buf = (qbuf, kbuf, vbuf)[kind]
        ref = chunk(buf, r if kind > 0 else 0, group)
        pltpu.make_async_copy(ref, ref, xch_recv.at[kind, group]).wait()

    def ring_copy(kind, group, way, send_at, r_at, peer):
        ref = chunk((kbuf, vbuf)[kind], r_at, group)
        return pltpu.make_async_remote_copy(
            src_ref=ref, dst_ref=ref,
            send_sem=ring_send.at[group, kind, send_at], recv_sem=ring_recv.at[group, kind, way],
            device_id=peer, device_id_type=MESH,
        )

    def ring_start(group):
        for kind in range(2):
            ring_copy(kind, group, 0, 0, r, right).start()
            ring_copy(kind, group, 1, 1, r, left).start()

    r_left, r_right, r_far = lax.rem(r + 3, 4), lax.rem(r + 1, 4), lax.rem(r + 2, 4)

    def ring_wait(kind, group, way):
        r_at = (r_left, r_right, r_far)[way]
        ref = chunk((kbuf, vbuf)[kind], r_at, group)
        pltpu.make_async_copy(ref, ref, ring_recv.at[group, kind, way]).wait()

    def ring_near(group):
        ring_wait(0, group, 0)
        ring_copy(0, group, 2, 2, r_left, right).start()
        ring_wait(1, group, 1)
        ring_copy(1, group, 2, 2, r_right, left).start()
        ring_wait(1, group, 0)
        ring_wait(0, group, 1)

    def ring_far(group):
        ring_wait(0, group, 2)
        ring_wait(1, group, 2)

    def tile(q_group, r_at, k_group, size, mask=None, tall=1):
        rows = pl.ds(pl.multiple_of(q_group * GRP, GRP), tall * GRP)
        keys = pl.ds(pl.multiple_of(r_at * (4 * GRP) + k_group * GRP, GRP), size)
        scores = lax.dot_general(
            qbuf[rows, :], kbuf[keys, :], (((1,), (1,)), ((), ())), preferred_element_type=jnp.float32
        )
        if mask is not None:
            scores = jnp.where(mask, scores, LOW)
        old = m_ref[rows, :]
        new = jnp.maximum(old, jnp.max(scores, axis=1, keepdims=True))
        m_ref[rows, :] = new
        keep = jnp.exp2((old - new) * SCALE)
        shift = new * SCALE
        weights = jnp.exp2(scores * SCALE - jnp.concatenate([shift] * (size // HS), axis=1))
        total = weights[:, :HS]
        for at in range(1, size // HS):
            total = total + weights[:, at * HS:(at + 1) * HS]
        l_ref[rows, :] = l_ref[rows, :] * keep + total
        acc_ref[rows, :] = acc_ref[rows, :] * keep + jnp.dot(
            weights.astype(jnp.bfloat16), vbuf[keys, :], preferred_element_type=jnp.float32
        )

    def own_tile(group):
        row = lax.broadcasted_iota(jnp.int32, (GRP, GRP), 0)
        column = lax.broadcasted_iota(jnp.int32, (GRP, GRP), 1)
        tile(group, r, group, GRP, column <= row)

    def other_tile(group, r_at):
        before = jnp.where((r_at < r) == (group < 2), 1, 0)

        @pl.when((core == 1) | (before == 1))
        def _():
            row = lax.broadcasted_iota(jnp.int32, (GRP, GRP), 0) // BLK
            column = lax.broadcasted_iota(jnp.int32, (GRP, GRP), 1) // BLK
            count = row * jnp.where(core == 0, 0, 1) + jnp.where(core == 0, 4, 1) * before
            tile(group, r_at, group, GRP, column < count)

    def low_keys(r_at):
        tile(2, r_at, 0, 2 * GRP, tall=2)

    def finish(group):
        rows = pl.ds(group * GRP, GRP)
        total = jnp.sum(l_ref[rows, :], axis=1, keepdims=True)
        obuf[rows, :] = (acc_ref[rows, :] / total).astype(jnp.bfloat16)
        half = group // 2
        z_at = group if half == 0 else 3 - group
        column = pl.multiple_of((z * 4 + w) * HS, HS)
        dst = att.at[pl.ds(half * BLK, BLK), pl.ds(column, HS)]
        for dw in (1, 2, 3, 0):
            w_at = lax.rem(w + dw, 4)
            slot = w_at if half == 0 else 3 - w_at
            src = obuf.at[pl.ds(pl.multiple_of(group * GRP + slot * BLK, BLK), BLK), :]

            def remote(src=src, w_at=w_at, dw=dw):
                return pltpu.make_async_remote_copy(
                    src_ref=src, dst_ref=dst,
                    send_sem=ret_send.at[group, dw], recv_sem=ret_recv.at[half],
                    device_id=device(z_at, r, w_at), device_id_type=MESH,
                )

            if dw == 0:
                @pl.when(z == z_at)
                def _():
                    pltpu.make_async_copy(src, dst, ret_recv.at[half]).start()

                @pl.when(z != z_at)
                def _():
                    remote().start()
            else:
                remote().start()

    def returned_sent(group):
        half = group // 2
        z_at = group if half == 0 else 3 - group
        for dw in range(4):
            ref = obuf.at[pl.ds(0, BLK), :]
            if dw == 0:
                @pl.when(z != z_at)
                def _():
                    pltpu.make_async_copy(ref, ref, ret_send.at[group, dw]).wait()
            else:
                pltpu.make_async_copy(ref, ref, ret_send.at[group, dw]).wait()

    def project(half, tp_at, at):
        column = pl.multiple_of(tp_at * OUT + at * PIECE, PIECE)
        return jnp.dot(
            att[pl.ds(half * BLK, BLK), :], wbuf[:, pl.ds(column, PIECE)], preferred_element_type=jnp.float32
        )

    def piece(buf, *lead):
        *lead, at = lead
        return buf.at[(*lead, slice(None), pl.ds(pl.multiple_of(at * PIECE, PIECE), PIECE))]

    def give_copy(half, which, at):
        return pltpu.make_async_remote_copy(
            src_ref=piece(give, half, which, at), dst_ref=piece(got, half, which, at),
            send_sem=give_send.at[half, which, at], recv_sem=give_recv.at[half, which, at],
            device_id=twin, device_id_type=MESH,
        )

    def far_copy(half, at):
        return pltpu.make_async_remote_copy(
            src_ref=piece(far_give, half, at), dst_ref=piece(far_got, half, at),
            send_sem=far_send.at[half, at], recv_sem=far_recv.at[half, at],
            device_id=far, device_id_type=MESH,
        )

    def project_give(half, which):
        tp_at = lax.rem(twin[1] + (2 if which == 0 else 0), 4)

        @pl.loop(0, PIECES)
        def _(at):
            piece(give, half, which, at)[...] = project(half, tp_at, at).astype(jnp.bfloat16)
            give_copy(half, which, at).start()

    def project_far(half):
        @pl.loop(0, PIECES)
        def _(at):
            own = project(half, far[1], at)
            give_copy(half, 0, at).wait_recv()
            piece(far_give, half, at)[...] = (own + piece(got, half, 0, at)[...].astype(jnp.float32)).astype(jnp.bfloat16)
            far_copy(half, at).start()

    def project_home(half):
        @pl.loop(0, PIECES)
        def _(at):
            own = project(half, tp, at)
            give_copy(half, 1, at).wait_recv()
            piece(home, half, at)[...] = own + piece(got, half, 1, at)[...].astype(jnp.float32)

    def project_end(half):
        @pl.loop(0, PIECES)
        def _(at):
            far_copy(half, at).wait_recv()
            both = piece(home, half, at)[...] + piece(far_got, half, at)[...].astype(jnp.float32)
            columns = pl.ds(pl.multiple_of(at * PIECE, PIECE), PIECE)
            out_ref[pl.ds(half * BLK, BLK), columns] = both.astype(jnp.bfloat16)

    def returned(half):
        ref = att.at[pl.ds(half * BLK, BLK), :]
        pltpu.make_async_copy(ref, ref, ret_recv.at[half]).wait()

    exchange(1, 0)
    exchange(2, 0)
    load_w = pltpu.make_async_copy(w_in, wbuf, w_sem)
    load_w.start()

    m_ref[...] = jnp.full_like(m_ref, LOW)
    l_ref[...] = jnp.zeros_like(l_ref)
    acc_ref[...] = jnp.zeros_like(acc_ref)

    def exchanged_start(group):
        exchanged(1, group)
        exchanged(2, group)
        ring_start(group)

    def low(r_at):
        other_tile(0, r_at)
        tile(1, r_at, 0, GRP)
        other_tile(1, r_at)

    def high(r_at):
        other_tile(2, r_at)
        tile(3, r_at, 2, GRP)
        other_tile(3, r_at)

    first, second, third, fourth = z, 1 - z, 3 - z, 2 + z

    exchanged_start(first)
    exchange(0, 0)
    exchanged_start(second)
    exchange(1, 1)
    exchange(2, 1)
    exchanged(0, 0)
    exchanged(0, 1)
    exchange(0, 1)
    own_tile(0)
    tile(1, r, 0, GRP)
    own_tile(1)
    ring_near(first)
    ring_near(second)
    exchanged_start(third)

    @pl.loop(0, 2)
    def _(at):
        low(lax.rem(r + 3 + 2 * at, 4))

    exchanged_start(fourth)
    ring_far(first)
    ring_far(second)
    low(r_far)
    finish(0)
    finish(1)
    exchanged(0, 2)
    exchanged(0, 3)

    @pl.loop(0, 2)
    def _(at):
        low_keys(lax.rem(r + 3 * at, 4))

    ring_near(third)

    low_keys(r_right)
    ring_near(fourth)
    load_w.wait()
    returned(0)
    project_give(0, 0)
    project_far(0)
    low_keys(r_far)
    own_tile(2)
    tile(3, r, 2, GRP)
    own_tile(3)

    @pl.loop(0, 2)
    def _(at):
        high(lax.rem(r + 3 + 2 * at, 4))

    ring_far(third)
    ring_far(fourth)
    high(r_far)
    finish(2)
    finish(3)
    project_give(0, 1)
    project_home(0)
    returned(1)
    project_give(1, 0)
    project_far(1)
    project_give(1, 1)
    project_home(1)
    project_end(0)
    project_end(1)

    for kind in range(3):
        for half in range(2):
            exchange_sent(kind, half)
    for group in range(4):
        returned_sent(group)
        for kind in range(2):
            for at in range(3):
                ref = chunk(kbuf, 0, group)
                pltpu.make_async_copy(ref, ref, ring_send.at[group, kind, at]).wait()
    for half in range(2):
        for at in range(PIECES):
            give_copy(half, 0, at).wait_send()
            give_copy(half, 1, at).wait_send()
            far_copy(half, at).wait_send()


def body(queries, attn_keys, attn_values, out_proj):
    tokens, inner = queries.shape
    any_spec = pl.BlockSpec(memory_space=pl.ANY)
    return pl.pallas_call(
        block_kernel,
        out_shape=jax.ShapeDtypeStruct((tokens, OUT), jnp.bfloat16),
        in_specs=[any_spec] * 4,
        out_specs=pl.BlockSpec(memory_space=pltpu.VMEM),
        scratch_shapes=[
            pltpu.VMEM((4 * GRP, HS), jnp.bfloat16),
            pltpu.VMEM((16 * GRP, HS), jnp.bfloat16),
            pltpu.VMEM((16 * GRP, HS), jnp.bfloat16),
            pltpu.VMEM((4 * GRP, HS), jnp.float32),
            pltpu.VMEM((4 * GRP, HS), jnp.float32),
            pltpu.VMEM((4 * GRP, HS), jnp.float32),
            pltpu.VMEM((4 * GRP, HS), jnp.bfloat16),
            pltpu.VMEM((tokens, inner), jnp.bfloat16),
            pltpu.VMEM((inner, 4 * OUT), jnp.bfloat16),
            pltpu.VMEM((2, 2, BLK, OUT), jnp.bfloat16),
            pltpu.VMEM((2, 2, BLK, OUT), jnp.bfloat16),
            pltpu.VMEM((2, BLK, OUT), jnp.bfloat16),
            pltpu.VMEM((2, BLK, OUT), jnp.bfloat16),
            pltpu.VMEM((2, BLK, OUT), jnp.float32),
            pltpu.SemaphoreType.DMA((3, 2)),
            pltpu.SemaphoreType.DMA((3, 4)),
            pltpu.SemaphoreType.DMA((4, 2, 3)),
            pltpu.SemaphoreType.DMA((4, 2, 3)),
            pltpu.SemaphoreType.DMA((4, 4)),
            pltpu.SemaphoreType.DMA((2,)),
            pltpu.SemaphoreType.DMA((2, 2, PIECES)),
            pltpu.SemaphoreType.DMA((2, 2, PIECES)),
            pltpu.SemaphoreType.DMA((2, PIECES)),
            pltpu.SemaphoreType.DMA((2, PIECES)),
            pltpu.SemaphoreType.DMA,
        ],
        compiler_params=pltpu.CompilerParams(
            collective_id=0, has_side_effects=True, vmem_limit_bytes=60 * 2**20
        ),
    )(queries, attn_keys, attn_values, out_proj)


def solution(mesh):
    in_specs = (P("ctx", "tp"), P("ctx", "tp"), P("ctx", "tp"), P("tp", None))
    out_specs = P("ctx", "tp")
    return jax.shard_map(body, mesh=mesh, in_specs=in_specs, out_specs=out_specs, check_vma=False)
```

```python
import functools

import jax
import jax.numpy as jnp
from jax import lax
from jax.experimental import pallas as pl
from jax.experimental.pallas import tpu as pltpu
from jax.sharding import PartitionSpec as P

MESH = pl.DeviceIdType.MESH
HS = 128
BLK = 128
GRP = 512
SCALE = 1.4426950408889634 / HS**0.5
LOW = -1e30
OUT = 2048
PIECE = 1024
PIECES = OUT // PIECE


def block_kernel(
    q_in, k_in, v_in, w_in, out_ref,
    qbuf, kbuf, vbuf, m_ref, l_ref, acc_ref, obuf, att, wbuf, give, got, far_give, far_got, home,
    xch_send, xch_recv, ring_send, ring_recv, ret_send, ret_recv,
    give_send, give_recv, far_send, far_recv, w_sem,
):
    ctx = lax.axis_index("ctx")
    tp = lax.axis_index("tp")
    core = lax.rem(tp, 2)
    z, a, b = ctx // 16, lax.rem(ctx // 4, 4), lax.rem(ctx, 4)
    r = jnp.where(core == 0, a, b)
    w = jnp.where(core == 0, b, a)

    def device(z_at, r_at, w_at):
        at = z_at * 16 + jnp.where(core == 0, r_at * 4 + w_at, w_at * 4 + r_at)
        return (at, tp)

    left = device(z, lax.rem(r + 3, 4), w)
    right = device(z, lax.rem(r + 1, 4), w)
    spread = [(dz, dw) for dz in range(2) for dw in range(4)]

    def spread_at(dz, dw):
        return lax.rem(z + dz, 2), lax.rem(w + dw, 4)

    barrier = pltpu.get_barrier_semaphore()
    for dz, dw in spread[1:]:
        z_at, w_at = spread_at(dz, dw)
        pl.semaphore_signal(barrier, inc=1, device_id=device(z_at, r, w_at), device_id_type=MESH)
    for peer in (left, right):
        pl.semaphore_signal(barrier, inc=1, device_id=peer, device_id_type=MESH)
    twin = (ctx, tp + 1 - 2 * core)
    far = (ctx, lax.rem(tp + 2, 4))
    for peer in (twin, far):
        pl.semaphore_signal(barrier, inc=1, device_id=peer, device_id_type=MESH)
    load_w = pltpu.make_async_copy(w_in, wbuf, w_sem)
    load_w.start()
    m_ref[...] = jnp.full_like(m_ref, LOW)
    l_ref[...] = jnp.zeros_like(l_ref)
    acc_ref[...] = jnp.zeros_like(acc_ref)
    pl.semaphore_wait(barrier, len(spread) + 3)

    ins = (q_in, k_in, v_in)

    def exchange(kind, half):
        group = z if half == 0 else 3 - z
        slot = w if half == 0 else 3 - w
        base = group * GRP + slot * BLK
        if kind > 0:
            base = base + r * (4 * GRP)
        dst = (qbuf, kbuf, vbuf)[kind].at[pl.ds(pl.multiple_of(base, BLK), BLK), :]
        for dz, dw in spread[4:] + spread[1:4] + spread[:1]:
            z_at, w_at = spread_at(dz, dw)
            column = pl.multiple_of((z_at * 4 + w_at) * HS, HS)
            src = ins[kind].at[pl.ds(half * BLK, BLK), pl.ds(column, HS)]
            if (dz, dw) == (0, 0):
                pltpu.make_async_copy(src, dst, xch_recv.at[kind, group]).start()
            else:
                pltpu.make_async_remote_copy(
                    src_ref=src, dst_ref=dst,
                    send_sem=xch_send.at[kind, half], recv_sem=xch_recv.at[kind, group],
                    device_id=device(z_at, r, w_at), device_id_type=MESH,
                ).start()

    def exchange_sent(kind, half):
        ref = ins[kind].at[pl.ds(half * BLK, BLK), pl.ds(0, 7 * HS)]
        pltpu.make_async_copy(ref, ref, xch_send.at[kind, half]).wait()

    def chunk(buf, r_at, group):
        return buf.at[pl.ds(pl.multiple_of(r_at * (4 * GRP) + group * GRP, GRP), GRP), :]

    def exchanged(kind, group):
        buf = (qbuf, kbuf, vbuf)[kind]
        ref = chunk(buf, r if kind > 0 else 0, group)
        pltpu.make_async_copy(ref, ref, xch_recv.at[kind, group]).wait()

    def ring_copy(kind, group, way, send_at, r_at, peer):
        ref = chunk((kbuf, vbuf)[kind], r_at, group)
        return pltpu.make_async_remote_copy(
            src_ref=ref, dst_ref=ref,
            send_sem=ring_send.at[group, kind, send_at], recv_sem=ring_recv.at[group, kind, way],
            device_id=peer, device_id_type=MESH,
        )

    def ring_start(group):
        for kind in range(2):
            ring_copy(kind, group, 0, 0, r, right).start()
            ring_copy(kind, group, 1, 1, r, left).start()

    r_left, r_right, r_far = lax.rem(r + 3, 4), lax.rem(r + 1, 4), lax.rem(r + 2, 4)

    def ring_wait(kind, group, way):
        r_at = (r_left, r_right, r_far)[way]
        ref = chunk((kbuf, vbuf)[kind], r_at, group)
        pltpu.make_async_copy(ref, ref, ring_recv.at[group, kind, way]).wait()

    def ring_near(group):
        ring_wait(0, group, 0)
        ring_copy(0, group, 2, 2, r_left, right).start()
        ring_wait(1, group, 1)
        ring_copy(1, group, 2, 2, r_right, left).start()
        ring_wait(1, group, 0)
        ring_wait(0, group, 1)

    def ring_far(group):
        ring_wait(0, group, 2)
        ring_wait(1, group, 2)

    def tile(q_group, r_at, k_group, size, mask=None, tall=1):
        rows = pl.ds(pl.multiple_of(q_group * GRP, GRP), tall * GRP)
        keys = pl.ds(pl.multiple_of(r_at * (4 * GRP) + k_group * GRP, GRP), size)
        scores = lax.dot_general(
            qbuf[rows, :], kbuf[keys, :], (((1,), (1,)), ((), ())), preferred_element_type=jnp.float32
        )
        if mask is not None:
            scores = jnp.where(mask, scores, LOW)
        old = m_ref[rows, :]
        new = jnp.maximum(old, jnp.max(scores, axis=1, keepdims=True))
        m_ref[rows, :] = new
        keep = jnp.exp2((old - new) * SCALE)
        shift = new * SCALE
        weights = jnp.exp2(scores * SCALE - jnp.concatenate([shift] * (size // HS), axis=1))
        total = weights[:, :HS]
        for at in range(1, size // HS):
            total = total + weights[:, at * HS:(at + 1) * HS]
        l_ref[rows, :] = l_ref[rows, :] * keep + total
        acc_ref[rows, :] = acc_ref[rows, :] * keep + jnp.dot(
            weights.astype(jnp.bfloat16), vbuf[keys, :], preferred_element_type=jnp.float32
        )

    def own_tile(group):
        row = lax.broadcasted_iota(jnp.int32, (GRP, GRP), 0)
        column = lax.broadcasted_iota(jnp.int32, (GRP, GRP), 1)
        tile(group, r, group, GRP, column <= row)

    def other_tile(group, r_at):
        before = jnp.where((r_at < r) == (group < 2), 1, 0)

        @pl.when((core == 1) | (before == 1))
        def _():
            row = lax.broadcasted_iota(jnp.int32, (GRP, GRP), 0) // BLK
            column = lax.broadcasted_iota(jnp.int32, (GRP, GRP), 1) // BLK
            count = row * jnp.where(core == 0, 0, 1) + jnp.where(core == 0, 4, 1) * before
            tile(group, r_at, group, GRP, column < count)

    def low_keys(r_at):
        tile(2, r_at, 0, 2 * GRP, tall=2)

    def finish(group):
        rows = pl.ds(group * GRP, GRP)
        total = jnp.sum(l_ref[rows, :], axis=1, keepdims=True)
        obuf[rows, :] = (acc_ref[rows, :] / total).astype(jnp.bfloat16)
        half = group // 2
        z_at = group if half == 0 else 3 - group
        column = pl.multiple_of((z * 4 + w) * HS, HS)
        dst = att.at[pl.ds(half * BLK, BLK), pl.ds(column, HS)]
        for dw in (1, 2, 3, 0):
            w_at = lax.rem(w + dw, 4)
            slot = w_at if half == 0 else 3 - w_at
            src = obuf.at[pl.ds(pl.multiple_of(group * GRP + slot * BLK, BLK), BLK), :]

            def remote(src=src, w_at=w_at, dw=dw):
                return pltpu.make_async_remote_copy(
                    src_ref=src, dst_ref=dst,
                    send_sem=ret_send.at[group, dw], recv_sem=ret_recv.at[half],
                    device_id=device(z_at, r, w_at), device_id_type=MESH,
                )

            if dw == 0:
                @pl.when(z == z_at)
                def _():
                    pltpu.make_async_copy(src, dst, ret_recv.at[half]).start()

                @pl.when(z != z_at)
                def _():
                    remote().start()
            else:
                remote().start()

    def returned_sent(group):
        half = group // 2
        z_at = group if half == 0 else 3 - group
        for dw in range(4):
            ref = obuf.at[pl.ds(0, BLK), :]
            if dw == 0:
                @pl.when(z != z_at)
                def _():
                    pltpu.make_async_copy(ref, ref, ret_send.at[group, dw]).wait()
            else:
                pltpu.make_async_copy(ref, ref, ret_send.at[group, dw]).wait()

    def project(half, tp_at, at):
        column = pl.multiple_of(tp_at * OUT + at * PIECE, PIECE)
        return jnp.dot(
            att[pl.ds(half * BLK, BLK), :], wbuf[:, pl.ds(column, PIECE)], preferred_element_type=jnp.float32
        )

    def piece(buf, *lead):
        *lead, at = lead
        return buf.at[(*lead, slice(None), pl.ds(pl.multiple_of(at * PIECE, PIECE), PIECE))]

    def give_copy(half, which, at):
        return pltpu.make_async_remote_copy(
            src_ref=piece(give, half, which, at), dst_ref=piece(got, half, which, at),
            send_sem=give_send.at[half, which, at], recv_sem=give_recv.at[half, which, at],
            device_id=twin, device_id_type=MESH,
        )

    def far_copy(half, at):
        return pltpu.make_async_remote_copy(
            src_ref=piece(far_give, half, at), dst_ref=piece(far_got, half, at),
            send_sem=far_send.at[half, at], recv_sem=far_recv.at[half, at],
            device_id=far, device_id_type=MESH,
        )

    def project_give(half, which):
        tp_at = lax.rem(twin[1] + (2 if which == 0 else 0), 4)

        @pl.loop(0, PIECES)
        def _(at):
            piece(give, half, which, at)[...] = project(half, tp_at, at).astype(jnp.bfloat16)
            give_copy(half, which, at).start()

    def project_far(half):
        @pl.loop(0, PIECES)
        def _(at):
            own = project(half, far[1], at)
            give_copy(half, 0, at).wait_recv()
            piece(far_give, half, at)[...] = (own + piece(got, half, 0, at)[...].astype(jnp.float32)).astype(jnp.bfloat16)
            far_copy(half, at).start()

    def project_home(half):
        @pl.loop(0, PIECES)
        def _(at):
            own = project(half, tp, at)
            give_copy(half, 1, at).wait_recv()
            piece(home, half, at)[...] = own + piece(got, half, 1, at)[...].astype(jnp.float32)

    def project_end(half):
        @pl.loop(0, PIECES)
        def _(at):
            far_copy(half, at).wait_recv()
            both = piece(home, half, at)[...] + piece(far_got, half, at)[...].astype(jnp.float32)
            columns = pl.ds(pl.multiple_of(at * PIECE, PIECE), PIECE)
            out_ref[pl.ds(half * BLK, BLK), columns] = both.astype(jnp.bfloat16)

    def returned(half):
        ref = att.at[pl.ds(half * BLK, BLK), :]
        pltpu.make_async_copy(ref, ref, ret_recv.at[half]).wait()

    exchange(1, 0)
    exchange(2, 0)

    def exchanged_start(group):
        exchanged(1, group)
        exchanged(2, group)
        ring_start(group)

    def low(r_at):
        other_tile(0, r_at)
        tile(1, r_at, 0, GRP)
        other_tile(1, r_at)

    def high(r_at):
        other_tile(2, r_at)
        tile(3, r_at, 2, GRP)
        other_tile(3, r_at)

    first, second, third, fourth = z, 1 - z, 3 - z, 2 + z

    exchanged_start(first)
    exchange(0, 0)
    exchanged_start(second)
    exchange(1, 1)
    exchange(2, 1)
    exchanged(0, 0)
    exchanged(0, 1)
    exchange(0, 1)
    own_tile(0)
    tile(1, r, 0, GRP)
    own_tile(1)
    ring_near(first)
    ring_near(second)
    exchanged_start(third)

    @pl.loop(0, 2)
    def _(at):
        low(lax.rem(r + 3 + 2 * at, 4))

    exchanged_start(fourth)
    ring_far(first)
    ring_far(second)
    low(r_far)
    finish(0)
    finish(1)
    exchanged(0, 2)
    exchanged(0, 3)

    @pl.loop(0, 2)
    def _(at):
        low_keys(lax.rem(r + 3 * at, 4))

    ring_near(third)

    low_keys(r_right)
    ring_near(fourth)
    load_w.wait()
    returned(0)
    project_give(0, 0)
    project_far(0)
    low_keys(r_far)
    own_tile(2)
    tile(3, r, 2, GRP)
    own_tile(3)

    @pl.loop(0, 2)
    def _(at):
        high(lax.rem(r + 3 + 2 * at, 4))

    ring_far(third)
    ring_far(fourth)
    high(r_far)
    finish(2)
    finish(3)
    project_give(0, 1)
    project_home(0)
    returned(1)
    project_give(1, 0)
    project_far(1)
    project_give(1, 1)
    project_home(1)
    project_end(0)
    project_end(1)

    for kind in range(3):
        for half in range(2):
            exchange_sent(kind, half)
    for group in range(4):
        returned_sent(group)
        for kind in range(2):
            for at in range(3):
                ref = chunk(kbuf, 0, group)
                pltpu.make_async_copy(ref, ref, ring_send.at[group, kind, at]).wait()
    for half in range(2):
        for at in range(PIECES):
            give_copy(half, 0, at).wait_send()
            give_copy(half, 1, at).wait_send()
            far_copy(half, at).wait_send()


def body(queries, attn_keys, attn_values, out_proj):
    tokens, inner = queries.shape
    any_spec = pl.BlockSpec(memory_space=pl.ANY)
    return pl.pallas_call(
        block_kernel,
        out_shape=jax.ShapeDtypeStruct((tokens, OUT), jnp.bfloat16),
        in_specs=[any_spec] * 4,
        out_specs=pl.BlockSpec(memory_space=pltpu.VMEM),
        scratch_shapes=[
            pltpu.VMEM((4 * GRP, HS), jnp.bfloat16),
            pltpu.VMEM((16 * GRP, HS), jnp.bfloat16),
            pltpu.VMEM((16 * GRP, HS), jnp.bfloat16),
            pltpu.VMEM((4 * GRP, HS), jnp.float32),
            pltpu.VMEM((4 * GRP, HS), jnp.float32),
            pltpu.VMEM((4 * GRP, HS), jnp.float32),
            pltpu.VMEM((4 * GRP, HS), jnp.bfloat16),
            pltpu.VMEM((tokens, inner), jnp.bfloat16),
            pltpu.VMEM((inner, 4 * OUT), jnp.bfloat16),
            pltpu.VMEM((2, 2, BLK, OUT), jnp.bfloat16),
            pltpu.VMEM((2, 2, BLK, OUT), jnp.bfloat16),
            pltpu.VMEM((2, BLK, OUT), jnp.bfloat16),
            pltpu.VMEM((2, BLK, OUT), jnp.bfloat16),
            pltpu.VMEM((2, BLK, OUT), jnp.float32),
            pltpu.SemaphoreType.DMA((3, 2)),
            pltpu.SemaphoreType.DMA((3, 4)),
            pltpu.SemaphoreType.DMA((4, 2, 3)),
            pltpu.SemaphoreType.DMA((4, 2, 3)),
            pltpu.SemaphoreType.DMA((4, 4)),
            pltpu.SemaphoreType.DMA((2,)),
            pltpu.SemaphoreType.DMA((2, 2, PIECES)),
            pltpu.SemaphoreType.DMA((2, 2, PIECES)),
            pltpu.SemaphoreType.DMA((2, PIECES)),
            pltpu.SemaphoreType.DMA((2, PIECES)),
            pltpu.SemaphoreType.DMA,
        ],
        compiler_params=pltpu.CompilerParams(
            collective_id=0, has_side_effects=True, vmem_limit_bytes=60 * 2**20
        ),
    )(queries, attn_keys, attn_values, out_proj)


def solution(mesh):
    in_specs = (P("ctx", "tp"), P("ctx", "tp"), P("ctx", "tp"), P("tp", None))
    out_specs = P("ctx", "tp")
    return jax.shard_map(body, mesh=mesh, in_specs=in_specs, out_specs=out_specs, check_vma=False)
```
